256 devices in a mesh: section: 16 (over x, y_hi, core), fsdp: 16 (over y_lo, z).
Axes of the slice: x: 4, y: 4 (y_hi: 2, y_lo: 2; y = y_hi * 2 + y_lo), z: 8, core: 2. Of those that a mesh axis runs over, the one named last changes fastest.
Arguments:
- text_states: bfloat16 [16, 256, 8192], P('fsdp'), may hold values from -6 to 6
- latents: bfloat16 [16, 512, 8192], P('fsdp', None, 'section'), may hold values from -68 to 68
- norm_gain: float32 [8192], replicated, may hold values from 0.5 to 1.5
- w_query: bfloat16 [8192, 8192], P('fsdp', 'section'), may hold values from -0.0625 to 0.0625
- w_key: bfloat16 [8192, 8192], P('fsdp', 'section'), may hold values from -0.0625 to 0.0625
- w_value: bfloat16 [8192, 8192], P('fsdp', 'section'), may hold values from -0.5 to 0.5
- w_out: bfloat16 [8192, 8192], P('section', 'fsdp'), may hold values from -0.09375 to 0.09375
- xattn_gate: float32 [1], replicated, may hold values from 0.5 to 1.5
- token_image: int32 [16, 256], P('fsdp'), may hold values from -1 to 7, as said below
Outputs:
- mixed_states: bfloat16 [16, 256, 8192], P('fsdp', None, 'section')
The draws below stay inside these ranges and needn't reach their ends.
Inputs may be any that keep to these rules, and one draw needn't show every extreme that they name: `token_image`: each row never falls from token to token; it is the number of image slots placed at or before the token, minus one.
All inputs are finite; a program needn't handle non-finite values.
Results may differ from the reference program's by a relative error of at most 0.007.
The reference program's roundings to bfloat16 on the way (of `normed`, `queries`, `keys`, `values`, `weights` and `attended`) count: a program that leaves them out, or rounds other values in their place, can miss the bound.
Values may be sent and summed in bfloat16 or wider, within the bound.
No kernel may reach another device: no remote copies, remote signals or barrier semaphores. Data moves between devices by JAX's collectives and lax.ppermute only.
A program may use at most 128 MiB of HBM per device.

```python
import jax
import jax.numpy as jnp
from jax import lax

D = 8192
HEADS = 64
HEAD_DIM = 128
LATENTS = 64
IMAGES = 8
TEXT_LEN = 256
SAMPLES = 16


def draw_latents(key, part):
    key = jax.random.fold_in(key, 1)
    array_shape = (SAMPLES, IMAGES * LATENTS, D)
    return jnp.clip(jax.random.normal(key, array_shape, jnp.float32), -6.0, 6.0).astype(jnp.bfloat16)


def draw_token_image(key, part):
    key = jax.random.fold_in(key, 2)
    count_key, place_key = jax.random.split(key)
    counts = jax.random.randint(count_key, (SAMPLES,), 1, IMAGES + 1)
    counts = jnp.where(jnp.arange(SAMPLES) == 0, IMAGES, counts)
    first_slot = TEXT_LEN // 16

    def place_images(one_key, one_count):
        picked = jax.random.permutation(one_key, TEXT_LEN - first_slot)[:IMAGES] + first_slot
        starts = jnp.where(jnp.arange(IMAGES) < one_count, picked, TEXT_LEN)
        starts = jnp.sort(starts)
        positions = jnp.arange(TEXT_LEN)
        return (jnp.sum((starts[None, :] <= positions[:, None]).astype(jnp.int32), axis=1) - 1).astype(jnp.int32)
    return jax.vmap(place_images)(jax.random.split(place_key, SAMPLES), counts)


def raised(values, key, source, target, parts, factor):
    def block_of(axis_at):
        return (jnp.arange(values.shape[axis_at]) // (values.shape[axis_at] // parts)).reshape((-1,) + (1,) * (values.ndim - 1 - axis_at))

    one_side = jax.random.permutation(key, parts)[block_of(target)]
    second = (block_of(target) + parts // 2) % parts
    return jnp.where((block_of(source) == one_side) | (block_of(source) == second), factor * values, values)


def shard_levels(rng, shape, shards, least, largest):
    gain, own = 1.0, jax.random.fold_in(rng, 6)
    for position, parts in shards:
        heights = jnp.exp(jax.random.uniform(jax.random.fold_in(own, position), (parts,), jnp.float32, least / len(shards), largest / len(shards)))
        gain = gain * jnp.repeat(heights, shape[position] // parts).reshape([-1 if axis == position else 1 for axis in range(len(shape))])
    return gain


def bell_draw(stream_key, dims, scale, reach, cuts=(), held_as=jnp.bfloat16):
    result = jax.random.normal(stream_key, dims, jnp.float32) * scale
    if len(cuts) > 0:
        result = shard_levels(stream_key, dims, cuts, -0.22, 0.18) * result
    return jnp.clip(result, min=-reach, max=reach).astype(held_as)


def heavy_noise(key, extent, width, most, cuts, heavy, held_as=jnp.bfloat16):
    result = width * jax.random.normal(key, extent, jnp.float32)
    if cuts:
        result = result * shard_levels(key, extent, cuts, -0.22, 0.18)
    return jnp.clip(raised(result, jax.random.fold_in(key, 3), *heavy), -most, most).astype(held_as)


def setup_inputs(seed: int = 0) -> dict:
    key_of = jax.random.split(jax.random.key(seed), 10)
    text_states = bell_draw(key_of[0], (SAMPLES, TEXT_LEN, D), 1.0, 6.0, ((0, 16),))
    latents = draw_latents(jax.random.fold_in(key_of[9], 71), 0)
    norm_gain = jnp.clip(1.0 + 0.1 * jax.random.normal(key_of[2], (D,), jnp.float32), 0.5, 1.5)
    w_query = bell_draw(key_of[3], (D, HEADS * HEAD_DIM), D ** -0.5, 0.0625, ((0, 16), (1, 16)))
    w_key = bell_draw(key_of[4], (D, HEADS * HEAD_DIM), D ** -0.5, 0.0625, ((0, 16), (1, 16)))
    w_value = bell_draw(key_of[5], (D, HEADS * HEAD_DIM), (D // 64) ** -0.5, 0.5, ((0, 16), (1, 16)))
    w_out = heavy_noise(key_of[6], (HEADS * HEAD_DIM, D), (HEADS * HEAD_DIM) ** -0.5, 0.09375, ((0, 16), (1, 16)), (0, 1, 16, 2.0))
    xattn_gate = jnp.clip(jax.random.uniform(key_of[7], (1,), jnp.float32, 0.5, 1.5), 0.5, 1.5)
    token_image = draw_token_image(jax.random.fold_in(key_of[9], 71), 0)
    return {"text_states": text_states, "latents": latents, "norm_gain": norm_gain, "w_query": w_query, "w_key": w_key, "w_value": w_value, "w_out": w_out, "xattn_gate": xattn_gate, "token_image": token_image}


def layer_norm(text_rows, norm_gain):
    values = text_rows.astype(jnp.float32)
    center = lax.optimization_barrier(jnp.mean(values, axis=-1, keepdims=True))
    spread = lax.optimization_barrier(jnp.mean(jnp.square(values - center), axis=-1, keepdims=True))
    return ((values - center) * lax.rsqrt(spread + 1e-05) * norm_gain.astype(jnp.float32)).astype(jnp.bfloat16)

def attend(queries, keys, values, image_rows):
    length = queries.shape[0]
    key_count = keys.shape[0]
    head_count = HEADS
    query_heads = queries.astype(jnp.float32).reshape(length, head_count, HEAD_DIM)
    key_heads = keys.astype(jnp.float32).reshape(key_count, head_count, HEAD_DIM)
    value_heads = values.astype(jnp.float32).reshape(key_count, head_count, HEAD_DIM)
    scores = jnp.einsum('lhd,rhd->hlr', query_heads, key_heads) * HEAD_DIM ** (-0.5)
    blocks = lax.broadcasted_iota(jnp.int32, (key_count,), 0) // LATENTS
    visible = (blocks[None, :] <= image_rows[:, None])[None, :, :]
    masked = jnp.where(visible, scores, -1e+30)
    row_top = lax.optimization_barrier(jnp.max(masked, axis=-1, keepdims=True))
    has_image = jnp.any(visible, axis=-1, keepdims=True)
    row_top = jnp.where(has_image, row_top, 0.0)
    exp_terms = jnp.where(visible, jnp.exp(masked - row_top), 0.0)
    denominator = lax.optimization_barrier(jnp.sum(exp_terms, axis=-1, keepdims=True))
    weights = (exp_terms / jnp.maximum(denominator, 1.0)).astype(jnp.bfloat16)
    attended = jnp.einsum('hlr,rhd->lhd', weights.astype(jnp.float32), value_heads)
    return attended.astype(jnp.bfloat16).reshape(length, head_count * HEAD_DIM)

def reference(text_states, latents, norm_gain, w_query, w_key, w_value, w_out, xattn_gate, token_image):

    def one_sample(inputs):
        text_rows, latent_rows, image_rows = inputs
        normed = layer_norm(text_rows, norm_gain)
        queries = jnp.dot(normed, w_query, preferred_element_type=jnp.float32).astype(jnp.bfloat16)
        keys = jnp.dot(latent_rows, w_key, preferred_element_type=jnp.float32).astype(jnp.bfloat16)
        values = jnp.dot(latent_rows, w_value, preferred_element_type=jnp.float32).astype(jnp.bfloat16)
        attended = attend(queries, keys, values, image_rows)
        projected = jnp.dot(attended, w_out, preferred_element_type=jnp.float32)
        mixed_rows = text_rows.astype(jnp.float32) + jnp.tanh(xattn_gate[0]) * projected
        return mixed_rows.astype(jnp.bfloat16)
    return lax.map(one_sample, (text_states, latents, token_image))
```

```python
import jax
import jax.numpy as jnp
from jax import lax
from jax.sharding import PartitionSpec as P

HEAD_DIM = 128
LATENTS = 64
AXES = ("section", "fsdp")
NX, NYH, NC, NYL, NZ = 4, 2, 2, 2, 8


def permute(value, place):
    pairs = []
    for x in range(NX):
        for yh in range(NYH):
            for c in range(NC):
                for yl in range(NYL):
                    for z in range(NZ):
                        tx, tyh, tc, tyl, tz = place(x, yh, c, yl, z)
                        pairs.append(
                            (
                                (x * 4 + yh * 2 + c) * 16 + yl * 8 + z,
                                (tx * 4 + tyh * 2 + tc) * 16 + tyl * 8 + tz,
                            )
                        )
    return lax.ppermute(value, AXES, pairs)


def swap_core_ylo(value):
    return permute(value, lambda x, yh, c, yl, z: (x, yh, yl, c, z))


def swap_core_xhi(value):
    return permute(value, lambda x, yh, c, yl, z: (c * 2 + x % 2, yh, x // 2, yl, z))


def swap_cores(value):
    return permute(value, lambda x, yh, c, yl, z: (x, yh, 1 - c, yl, z))


def over_x(value, r):
    return permute(value, lambda x, yh, c, yl, z: (x ^ r, yh, c, yl, z))


def over_y(value, q):
    return permute(value, lambda x, yh, c, yl, z: (x, yh ^ (q >> 1), c, yl ^ (q & 1), z))


def gather_z(value):
    groups = [list(range(NZ)), list(range(NZ, 2 * NZ))]
    return lax.all_gather(value, "fsdp", axis=0, tiled=True, axis_index_groups=groups)


def pick(stacked, index):
    return lax.dynamic_index_in_dim(stacked, index, 0, keepdims=False)


def layer_norm(text_rows, norm_gain):
    values = text_rows.astype(jnp.float32)
    center = jnp.mean(values, axis=-1, keepdims=True)
    spread = jnp.mean(jnp.square(values - center), axis=-1, keepdims=True)
    return ((values - center) * lax.rsqrt(spread + 1e-05) * norm_gain).astype(jnp.bfloat16)


def attention_weights(queries, keys, token_image):
    length, head_width = queries.shape
    key_count = keys.shape[0]
    head_count = head_width // HEAD_DIM
    query_heads = queries.reshape(length, head_count, HEAD_DIM)
    key_heads = keys.reshape(key_count, head_count, HEAD_DIM)
    scores = jnp.einsum(
        "lhd,rhd->hlr", query_heads, key_heads, preferred_element_type=jnp.float32
    ) * HEAD_DIM ** (-0.5)
    blocks = lax.broadcasted_iota(jnp.int32, (key_count,), 0) // LATENTS
    visible = (blocks[None, :] <= token_image[:, None])[None, :, :]
    masked = jnp.where(visible, scores, -1e30)
    row_top = jnp.max(masked, axis=-1, keepdims=True)
    has_image = jnp.any(visible, axis=-1, keepdims=True)
    row_top = jnp.where(has_image, row_top, 0.0)
    exp_terms = jnp.where(visible, jnp.exp(masked - row_top), 0.0)
    denominator = jnp.sum(exp_terms, axis=-1, keepdims=True)
    return (exp_terms / jnp.maximum(denominator, 1.0)).astype(jnp.bfloat16)


def attend(weights, values):
    key_count, head_width = values.shape
    value_heads = values.reshape(key_count, head_width // HEAD_DIM, HEAD_DIM)
    attended = jnp.einsum("hlr,rhd->lhd", weights, value_heads, preferred_element_type=jnp.float32)
    return attended.astype(jnp.bfloat16).reshape(-1, head_width)


def gather_plane(block, order):
    half = block.shape[0] // 2
    first, second = block[:half], block[half:]
    xs = jnp.stack([first] + [over_x(first, r) for r in (1, 2, 3)])
    ys = jnp.stack([second] + [over_y(second, q) for q in (1, 2, 3)])
    first_all = [xs] + [over_y(xs, q) for q in (1, 2, 3)]
    second_all = [ys] + [over_x(ys, r) for r in (1, 2, 3)]
    top = jnp.stack(first_all)
    low = jnp.stack(second_all)
    samples = []
    for t in range(2):
        parts_top, parts_low = [], []
        for b in range(8):
            e = order ^ b
            r = ((e >> 2) & 1) + 2 * (e & 1)
            q = 2 * ((e >> 1) & 1) + t
            parts_top.append(lax.dynamic_slice(top, (q, r, 0, 0), (1, 1) + top.shape[2:])[0, 0])
            parts_low.append(lax.dynamic_slice(low, (r, q, 0, 0), (1, 1) + low.shape[2:])[0, 0])
        samples.append(jnp.concatenate(parts_top, axis=1))
        samples.append(jnp.concatenate(parts_low, axis=1))
    return jnp.concatenate(samples, axis=0)


def reduce_x(parts, x):
    total = pick(parts, x)
    for r in (1, 2, 3):
        total = total + over_x(pick(parts, x ^ r).astype(jnp.bfloat16), r).astype(jnp.float32)
    return total


def reduce_y(parts, y):
    total = pick(parts, y)
    for q in (1, 2, 3):
        total = total + over_y(pick(parts, y ^ q).astype(jnp.bfloat16), q).astype(jnp.float32)
    return total


def body(text_states, latents, norm_gain, w_query, w_key, w_value, w_out, xattn_gate, token_image):
    _, length, model_width = text_states.shape
    key_count = latents.shape[1]
    section, place = lax.axis_index("section"), lax.axis_index("fsdp")
    x, yh, core, yl = section // 4, (section // 2) % 2, section % 2, place // NZ
    y = yh * 2 + yl
    keep = core ^ yl
    half_width = model_width // 2

    key_part = gather_z(swap_core_ylo(w_key))
    query_part = gather_z(swap_core_ylo(w_query))
    value_part = gather_z(swap_core_ylo(w_value))
    out_part = gather_z(swap_core_ylo(w_out))

    latent_rows = gather_plane(
        swap_core_xhi(latents[0]), (x % 2) * 4 + yh * 2 + x // 2
    )

    normed = layer_norm(text_states[0], norm_gain)
    own_half = lax.dynamic_slice_in_dim(normed, core * half_width, half_width, 1)
    text_rows = jnp.concatenate([own_half, over_y(own_half, 1)], axis=0)
    images = swap_core_ylo(token_image)[0]

    def project(rows, weight):
        sums = jnp.dot(rows, weight, preferred_element_type=jnp.float32)
        sums = sums.reshape(2, rows.shape[0] // 2, weight.shape[1])
        return (pick(sums, keep) + swap_cores(pick(sums, 1 - keep))).astype(jnp.bfloat16)

    keys = project(latent_rows, key_part)
    queries = project(text_rows, query_part)
    weights = attention_weights(queries, keys, images)
    values = project(latent_rows, value_part)
    attended = attend(weights, values)
    other = swap_cores(attended)
    pair = jnp.stack([attended, other])
    pair = jnp.stack([pick(pair, core), pick(pair, 1 - core)])

    width = w_out.shape[1]
    out_blocks = out_part.reshape(NZ, -1, width)
    sums = []
    for c in range(2):
        for xl in range(2):
            for h in range(2):
                block = out_blocks[xl * 4 + h * 2 + c]
                sums.append(
                    jnp.einsum("jlk,kn->jln", pair, block, preferred_element_type=jnp.float32)
                )
    sums = jnp.stack(sums).reshape(4, 4, length, width)
    cut = length // 2
    first = reduce_y(reduce_x(sums[:, :, :cut], x), y)
    second = reduce_x(reduce_y(jnp.swapaxes(sums[:, :, cut:], 0, 1), y), x)
    projected = jnp.concatenate([first, second], axis=0)
    block_index = core * 8 + (x % 2) * 4 + yh * 2 + x // 2
    own_text = lax.dynamic_slice_in_dim(text_states[0], block_index * width, width, 1)
    mixed = own_text.astype(jnp.float32) + jnp.tanh(xattn_gate[0]) * projected
    return swap_core_xhi(mixed.astype(jnp.bfloat16))[None]


def solution(mesh):
    in_specs = (
        P("fsdp", None, None),
        P("fsdp", None, "section"),
        P(),
        P("fsdp", "section"),
        P("fsdp", "section"),
        P("fsdp", "section"),
        P("section", "fsdp"),
        P(),
        P("fsdp", None),
    )
    out_specs = P("fsdp", None, "section")
    return jax.shard_map(body, mesh=mesh, in_specs=in_specs, out_specs=out_specs, check_vma=False)
```

```python
import jax
import jax.numpy as jnp
from jax import lax
from jax.experimental import pallas as pl
from jax.experimental.pallas import tpu as pltpu
from jax.sharding import PartitionSpec as P

HEAD_DIM = 128
LATENTS = 64
AXES = ("section", "fsdp")
NX, NYH, NC, NYL, NZ = 4, 2, 2, 2, 8


def permute(value, place):
    pairs = []
    for x in range(NX):
        for yh in range(NYH):
            for c in range(NC):
                for yl in range(NYL):
                    for z in range(NZ):
                        tx, tyh, tc, tyl, tz = place(x, yh, c, yl, z)
                        pairs.append(
                            (
                                (x * 4 + yh * 2 + c) * 16 + yl * 8 + z,
                                (tx * 4 + tyh * 2 + tc) * 16 + tyl * 8 + tz,
                            )
                        )
    return lax.ppermute(value, AXES, pairs)


def to_parity(value):
    return permute(value, lambda x, yh, c, yl, z: (x, yh, z % 2, c, z ^ yl ^ c))


def swap_core_parity(value):
    return permute(value, lambda x, yh, c, yl, z: (x, yh, z % 2, yl, z // 2 * 2 + c))


def swap_cores(value):
    return permute(value, lambda x, yh, c, yl, z: (x, yh, 1 - c, yl, z))


def over_x(value, r):
    return permute(value, lambda x, yh, c, yl, z: (x ^ r, yh, c, yl, z))


def along_x(value, step):
    return permute(value, lambda x, yh, c, yl, z: ((x + step) % NX, yh, c, yl, z))


def over_y(value, q):
    return permute(value, lambda x, yh, c, yl, z: (x, yh ^ (q >> 1), c, yl ^ (q & 1), z))


def gather_z(value):
    groups = [list(range(NZ)), list(range(NZ, 2 * NZ))]
    return lax.all_gather(value, "fsdp", axis=0, axis_index_groups=groups)


def after(value, *earlier):
    return lax.optimization_barrier((value, *earlier))[0]


def gather_y(block):
    return jnp.stack([block] + [over_y(block, q) for q in (1, 2, 3)])


def gather_x(column):
    up, down = along_x(column, 1), along_x(column, -1)
    far = [along_x(up[:2], 1), along_x(down[2:], -1)]
    return jnp.concatenate([column, up, *far, down], axis=0)


def query_kernel(place_ref, own_ref, other_ref, weight_ref, kept, sent):
    @pl.when(pl.program_id(0) == 0)
    def _():
        kept[...] = jnp.zeros_like(kept)
        sent[...] = jnp.zeros_like(sent)

    weight = weight_ref[...]
    own = jnp.dot(own_ref[...], weight, preferred_element_type=jnp.float32)
    other = jnp.dot(other_ref[...], weight, preferred_element_type=jnp.float32)
    stays = place_ref[2] == place_ref[3]
    kept[...] += jnp.where(stays, own, other)
    sent[...] += jnp.where(stays, other, own)


def latent_kernel(place_ref, mine_ref, theirs_ref, weight_ref, kept, sent):
    @pl.when(pl.program_id(0) == 0)
    def _():
        kept[...] = jnp.zeros_like(kept)
        sent[...] = jnp.zeros_like(sent)

    for out, latent_ref in ((kept, mine_ref), (sent, theirs_ref)):
        latent = latent_ref[...]
        for n in range(2):
            out[n] += jnp.dot(latent, weight_ref[n], preferred_element_type=jnp.float32)


def weight_at(s, p):
    return s // 2 * 2 + ((s % 2) ^ p[2] ^ p[3])


def project_queries(place, normed, other_half, weights):
    length = normed.shape[0]
    steps, depth, width = weights.shape
    out = jax.ShapeDtypeStruct((length, width), jnp.float32)
    whole = pl.BlockSpec((length, width), lambda s, p: (0, 0))
    return pl.pallas_call(
        query_kernel,
        out_shape=(out, out),
        grid_spec=pltpu.PrefetchScalarGridSpec(
            num_scalar_prefetch=1,
            grid=(steps,),
            in_specs=[
                pl.BlockSpec((length, depth), lambda s, p: (0, (s % 2) * 8 + (s // 2) * 2 + p[2])),
                pl.BlockSpec((length, depth), lambda s, p: (0, (s % 2) * 4 + s // 2)),
                pl.BlockSpec((None, depth, width), lambda s, p: (weight_at(s, p), 0, 0)),
            ],
            out_specs=(whole, whole),
        ),
        compiler_params=pltpu.CompilerParams(vmem_limit_bytes=32 * 2**20),
        cost_estimate=pl.CostEstimate(
            flops=4 * length * steps * depth * width,
            bytes_accessed=2 * steps * depth * (2 * length + width) + 8 * length * width,
            transcendentals=0,
        ),
    )(place, normed, other_half, weights)


def project_latents(place, latent_blocks, weights):
    key_count = latent_blocks.shape[1]
    steps, kinds, depth, width = weights.shape

    def latent_spec(flip):
        def index(s, p):
            x_at, y_at = (s % 2) * 2 + s // 4, ((s // 2) % 2) * 2 + (p[2] + flip) % 2
            return (((p[0] - x_at + NX) % NX) * 4 + (y_at ^ p[1]), 0, 0)

        return pl.BlockSpec((None, key_count, depth), index)

    out = jax.ShapeDtypeStruct((kinds, key_count, width), jnp.float32)
    whole = pl.BlockSpec((kinds, key_count, width), lambda s, p: (0, 0, 0))
    return pl.pallas_call(
        latent_kernel,
        out_shape=(out, out),
        grid_spec=pltpu.PrefetchScalarGridSpec(
            num_scalar_prefetch=1,
            grid=(steps,),
            in_specs=[
                latent_spec(0),
                latent_spec(1),
                pl.BlockSpec((None, kinds, depth, width), lambda s, p: (weight_at(s, p), 0, 0, 0)),
            ],
            out_specs=(whole, whole),
        ),
        compiler_params=pltpu.CompilerParams(vmem_limit_bytes=40 * 2**20),
        cost_estimate=pl.CostEstimate(
            flops=4 * kinds * key_count * steps * depth * width,
            bytes_accessed=2 * steps * depth * (2 * key_count + kinds * width)
            + 8 * kinds * key_count * width,
            transcendentals=0,
        ),
    )(place, latent_blocks, latent_blocks, weights)


def out_kernel(place_ref, mine_ref, theirs_ref, block_ref, *parts):
    core, y_low, x_high = place_ref[2], place_ref[3], place_ref[0] // 2

    def product(ref):
        return (
            jnp.dot(ref[0], block_ref[y_low], preferred_element_type=jnp.float32)
            + jnp.dot(ref[1], block_ref[1 - y_low], preferred_element_type=jnp.float32)
        ).astype(jnp.bfloat16)

    mine, theirs = product(mine_ref), product(theirs_ref)
    near = jnp.where(core == x_high, mine, theirs)
    far = jnp.where(core == x_high, theirs, mine)
    for n in range(2):

        @pl.when(pl.program_id(0) // 2 == n)
        def _():
            parts[n][...] = near
            parts[2 + n][...] = far


def partial_sums(place, mine, theirs, blocks):
    _, length, depth = mine.shape
    steps, width = blocks.shape[0] // 2, blocks.shape[2]
    rows = pl.BlockSpec((2, length, depth), lambda s, p: (0, 0, 0))

    def block_index(s, p):
        return (((s // 2) ^ (p[0] % 2)) * 2 + ((s % 2) ^ (p[1] // 2)), 0, 0)

    def out_spec(n):
        def index(s, p):
            return (jnp.where(s // 2 == n, s % 2, jnp.where(s // 2 < n, 0, 1)), 0, 0)

        return pl.BlockSpec((None, length, width), index)

    return pl.pallas_call(
        out_kernel,
        out_shape=[jax.ShapeDtypeStruct((2, length, width), jnp.bfloat16)] * 4,
        grid_spec=pltpu.PrefetchScalarGridSpec(
            num_scalar_prefetch=1,
            grid=(steps,),
            in_specs=[rows, rows, pl.BlockSpec((2, depth, width), block_index)],
            out_specs=[out_spec(n % 2) for n in range(4)],
        ),
        compiler_params=pltpu.CompilerParams(vmem_limit_bytes=32 * 2**20),
        cost_estimate=pl.CostEstimate(
            flops=8 * length * depth * steps * width,
            bytes_accessed=2 * (4 * length * depth + 2 * steps * depth * width + 8 * length * width),
            transcendentals=0,
        ),
    )(place, mine, theirs, blocks)


def layer_norm(text_rows, norm_gain):
    values = text_rows.astype(jnp.float32)
    center = jnp.mean(values, axis=-1, keepdims=True)
    spread = jnp.mean(jnp.square(values - center), axis=-1, keepdims=True)
    return ((values - center) * lax.rsqrt(spread + 1e-05) * norm_gain).astype(jnp.bfloat16)


def attention_weights(queries, keys, token_image):
    length, head_width = queries.shape
    key_count = keys.shape[0]
    head_count = head_width // HEAD_DIM
    query_heads = queries.reshape(length, head_count, HEAD_DIM)
    key_heads = keys.reshape(key_count, head_count, HEAD_DIM)
    scores = jnp.einsum(
        "lhd,rhd->hlr", query_heads, key_heads, preferred_element_type=jnp.float32
    ) * HEAD_DIM ** (-0.5)
    blocks = lax.broadcasted_iota(jnp.int32, (key_count,), 0) // LATENTS
    visible = (blocks[None, :] <= token_image[:, None])[None, :, :]
    masked = jnp.where(visible, scores, -1e30)
    row_top = jnp.max(masked, axis=-1, keepdims=True)
    has_image = jnp.any(visible, axis=-1, keepdims=True)
    row_top = jnp.where(has_image, row_top, 0.0)
    exp_terms = jnp.where(visible, jnp.exp(masked - row_top), 0.0)
    denominator = jnp.sum(exp_terms, axis=-1, keepdims=True)
    return (exp_terms / jnp.maximum(denominator, 1.0)).astype(jnp.bfloat16)


def attend(weights, values):
    key_count, head_width = values.shape
    value_heads = values.reshape(key_count, head_width // HEAD_DIM, HEAD_DIM)
    attended = jnp.einsum("hlr,rhd->lhd", weights, value_heads, preferred_element_type=jnp.float32)
    return attended.astype(jnp.bfloat16).reshape(-1, head_width)


def to_final(piece, g):
    return permute(piece, lambda x, yh, c, yl, z: (yl * 2 + x % 2, yh ^ g, c, x // 2, z))


def total(own, moved):
    result = own.astype(jnp.float32)
    for part in moved:
        result = result + part.astype(jnp.float32)
    return result


def body(text_states, latents, norm_gain, w_query, w_key, w_value, w_out, xattn_gate, token_image):
    _, length, model_width = text_states.shape
    key_count = latents.shape[1]
    width = w_out.shape[1]
    section, place = lax.axis_index("section"), lax.axis_index("fsdp")
    x, yh, core, yl = section // 4, (section // 2) % 2, section % 2, place // NZ
    here = jnp.stack([x, yh * 2 + yl, core, yl]).astype(jnp.int32)

    latent_shard = to_parity(jnp.stack([w_key, w_value]))
    latent_weights = gather_z(latent_shard)
    column = gather_y(latents[0])
    latent_blocks = gather_x(column)
    query_shard = to_parity(after(w_query, column, latent_shard))
    query_weights = gather_z(query_shard)

    normed = layer_norm(text_states[0], norm_gain)
    own_half = jnp.concatenate(
        [lax.dynamic_slice_in_dim(normed, (2 * n + core) * width, width, 1) for n in range(NZ)], axis=1
    )
    other_half = over_y(after(own_half, query_shard), 1)
    out_shard = swap_core_parity(after(w_out, query_shard))
    out_blocks = gather_z(out_shard)
    other_image = over_y(after(token_image, out_shard), 1)
    images = jnp.where(core == yl, token_image, other_image)[0]

    kept, sent = project_queries(here, normed, other_half, query_weights)
    queries = (kept + swap_cores(sent)).astype(jnp.bfloat16)
    kept, sent = project_latents(here, latent_blocks, latent_weights)
    keys, values = (kept + swap_cores(sent)).astype(jnp.bfloat16)
    attended = attend(attention_weights(queries, keys, images), values)

    mine = jnp.stack([attended, over_y(attended, 1)])
    parts = partial_sums(here, mine, swap_cores(mine), out_blocks)
    near = total(parts[0], [over_x(parts[r], r) for r in (1, 2, 3)]).astype(jnp.bfloat16)
    projected = total(to_final(near[0], 0), [to_final(near[1], 1)])
    own_text = lax.dynamic_slice_in_dim(text_states[0], section * width, width, 1)
    mixed = own_text.astype(jnp.float32) + jnp.tanh(xattn_gate[0]) * projected
    return mixed.astype(jnp.bfloat16)[None]


def solution(mesh):
    in_specs = (
        P("fsdp", None, None),
        P("fsdp", None, "section"),
        P(),
        P("fsdp", "section"),
        P("fsdp", "section"),
        P("fsdp", "section"),
        P("section", "fsdp"),
        P(),
        P("fsdp", None),
    )
    out_specs = P("fsdp", None, "section")
    return jax.shard_map(body, mesh=mesh, in_specs=in_specs, out_specs=out_specs, check_vma=False)
```

```python
import jax
import jax.numpy as jnp
from jax import lax
from jax.experimental import pallas as pl
from jax.experimental.pallas import tpu as pltpu
from jax.sharding import PartitionSpec as P

HEAD_DIM = 128
LATENTS = 64
AXES = ("section", "fsdp")
NX, NYH, NC, NYL, NZ = 4, 2, 2, 2, 8


def permute(value, place):
    pairs = []
    for x in range(NX):
        for yh in range(NYH):
            for c in range(NC):
                for yl in range(NYL):
                    for z in range(NZ):
                        tx, tyh, tc, tyl, tz = place(x, yh, c, yl, z)
                        pairs.append(
                            (
                                (x * 4 + yh * 2 + c) * 16 + yl * 8 + z,
                                (tx * 4 + tyh * 2 + tc) * 16 + tyl * 8 + tz,
                            )
                        )
    return lax.ppermute(value, AXES, pairs)


def to_parity(value):
    return permute(value, lambda x, yh, c, yl, z: (x, yh, z % 2, c, z ^ yl ^ c))


def swap_core_parity(value):
    return permute(value, lambda x, yh, c, yl, z: (x, yh, z % 2, yl, z // 2 * 2 + c))


def swap_cores(value):
    return permute(value, lambda x, yh, c, yl, z: (x, yh, 1 - c, yl, z))


def over_x(value, r):
    return permute(value, lambda x, yh, c, yl, z: (x ^ r, yh, c, yl, z))


def along_x(value, step):
    return permute(value, lambda x, yh, c, yl, z: ((x + step) % NX, yh, c, yl, z))


def over_y(value, q):
    return permute(value, lambda x, yh, c, yl, z: (x, yh ^ (q >> 1), c, yl ^ (q & 1), z))


def pick(stacked, index):
    return lax.dynamic_index_in_dim(stacked, index, 0, keepdims=False)


def over_z(value, step):
    return permute(value, lambda x, yh, c, yl, z: (x, yh, c, yl, (z + step) % NZ))


def ring_z(shard):
    up, down = [shard], [shard]
    for _ in range(3):
        up.append(over_z(up[-1], 1))
        down.append(over_z(down[-1], -1))
    return down + [over_z(up[-1][:1], 1), over_z(down[-1][1:], -1)] + up[:0:-1]


def gather_z(value):
    groups = [list(range(NZ)), list(range(NZ, 2 * NZ))]
    return lax.all_gather(value, "fsdp", axis=0, axis_index_groups=groups)


def after(value, *earlier):
    return lax.optimization_barrier((value, *earlier))[0]


def gather_plane(block):
    groups = [
        [((y // 2) * 2 + x * 4 + core) * 16 + (y % 2) * NZ + z for x in range(NX) for y in range(4)]
        for z in range(NZ)
        for core in range(NC)
    ]
    return lax.all_gather(block, AXES, axis=0, axis_index_groups=groups)


def query_kernel(place_ref, own_ref, other_ref, weight_ref, kept, sent):
    @pl.when(pl.program_id(0) == 0)
    def _():
        kept[...] = jnp.zeros_like(kept)
        sent[...] = jnp.zeros_like(sent)

    weight = weight_ref[...]
    own = jnp.dot(own_ref[...], weight, preferred_element_type=jnp.float32)
    other = jnp.dot(other_ref[...], weight, preferred_element_type=jnp.float32)
    stays = place_ref[2] == place_ref[3]
    kept[...] += jnp.where(stays, own, other)
    sent[...] += jnp.where(stays, other, own)


def latent_kernel(place_ref, mine_0, mine_1, theirs_0, theirs_1, *refs):
    pieces, (kept, sent, held, sems) = refs[:9], refs[9:]
    k = pl.program_id(0)

    @pl.when(k == 0)
    def _():
        for n, piece in enumerate(pieces):
            if n in (4, 5):
                target, sem = held.at[4, pl.ds(n - 4, 1)], sems.at[4]
            else:
                target, sem = held.at[n - (n > 5)], sems.at[n - (n > 5)]
            pltpu.make_async_copy(piece, target, sem).start()

    at = []
    for j in range(2):
        d = (weight_at(2 * k + j, place_ref) - place_ref[4] + NZ) % NZ
        pltpu.make_async_copy(held.at[d], held.at[d], sems.at[d]).wait()
        at.append(d)
    for out, low, high in ((kept, mine_0, mine_1), (sent, theirs_0, theirs_1)):
        for n in range(2):
            sums = jnp.dot(low[...], held[at[0], n], preferred_element_type=jnp.float32) + jnp.dot(
                high[...], held[at[1], n], preferred_element_type=jnp.float32
            )

            @pl.when(k == 0)
            def _():
                out[n] = sums

            @pl.when(k > 0)
            def _():
                out[n] += sums


def weight_at(s, p):
    return s // 2 * 2 + ((s % 2) ^ p[2] ^ p[3])


def project_queries(place, normed, other_half, weights):
    length = normed.shape[1]
    steps, depth, width = weights.shape
    out = jax.ShapeDtypeStruct((length, width), jnp.float32)
    whole = pl.BlockSpec((length, width), lambda s, p: (0, 0))
    return pl.pallas_call(
        query_kernel,
        out_shape=(out, out),
        grid_spec=pltpu.PrefetchScalarGridSpec(
            num_scalar_prefetch=1,
            grid=(steps,),
            in_specs=[
                pl.BlockSpec((None, length, depth), lambda s, p: (p[2], 0, (s % 2) * 4 + s // 2)),
                pl.BlockSpec((length, depth), lambda s, p: (0, (s % 2) * 4 + s // 2)),
                pl.BlockSpec((None, depth, width), lambda s, p: (weight_at(s, p), 0, 0)),
            ],
            out_specs=(whole, whole),
        ),
        compiler_params=pltpu.CompilerParams(vmem_limit_bytes=56 * 2**20),
        cost_estimate=pl.CostEstimate(
            flops=4 * length * steps * depth * width,
            bytes_accessed=2 * steps * depth * (2 * length + width) + 8 * length * width,
            transcendentals=0,
        ),
    )(place, normed, other_half, weights)


def project_latents(place, latent_blocks, pieces):
    key_count = latent_blocks.shape[1]
    kinds, depth, width = pieces[0].shape

    def latent_spec(flip, j):
        def index(k, p):
            x_at, y_at = j * 2 + k // 2, (k % 2) * 2 + (p[2] + flip) % 2
            return (x_at * 4 + y_at, 0, 0)

        return pl.BlockSpec((None, key_count, depth), index)

    out = jax.ShapeDtypeStruct((kinds, key_count, width), jnp.float32)
    whole = pl.BlockSpec((kinds, key_count, width), lambda k, p: (0, 0, 0))
    return pl.pallas_call(
        latent_kernel,
        out_shape=(out, out),
        grid_spec=pltpu.PrefetchScalarGridSpec(
            num_scalar_prefetch=1,
            grid=(NZ // 2,),
            in_specs=[latent_spec(flip, j) for flip in range(2) for j in range(2)]
            + [pl.BlockSpec(memory_space=pl.ANY)] * len(pieces),
            out_specs=(whole, whole),
            scratch_shapes=[
                pltpu.VMEM((NZ, kinds, depth, width), jnp.bfloat16),
                pltpu.SemaphoreType.DMA((NZ,)),
            ],
        ),
        compiler_params=pltpu.CompilerParams(vmem_limit_bytes=56 * 2**20),
        cost_estimate=pl.CostEstimate(
            flops=4 * kinds * key_count * NZ * depth * width,
            bytes_accessed=2 * NZ * depth * (2 * key_count + kinds * width)
            + 8 * kinds * key_count * width,
            transcendentals=0,
        ),
    )(place, *[latent_blocks] * 4, *pieces)


def out_kernel(place_ref, mine_ref, theirs_ref, near_ref, far_ref, *parts):
    core, x_high = place_ref[2], place_ref[0] // 2

    def product(ref):
        return (
            jnp.dot(ref[0], near_ref[...], preferred_element_type=jnp.float32)
            + jnp.dot(ref[1], far_ref[...], preferred_element_type=jnp.float32)
        ).astype(jnp.bfloat16)

    mine, theirs = product(mine_ref), product(theirs_ref)
    near = jnp.where(core == x_high, mine, theirs)
    far = jnp.where(core == x_high, theirs, mine)
    for n in range(2):

        @pl.when(pl.program_id(0) // 2 == n)
        def _():
            parts[n][...] = near
            parts[2 + n][...] = far


def partial_sums(place, mine, theirs, blocks):
    _, length, depth = mine.shape
    steps, width = blocks.shape[0] // 2, blocks.shape[2]
    rows = pl.BlockSpec((2, length, depth), lambda s, p: (0, 0, 0))

    def block_spec(flip):
        def index(s, p):
            z = ((s // 2) ^ (p[0] % 2)) * 4 + ((s % 2) ^ (p[1] // 2)) * 2 + (p[3] ^ flip)
            return (z, 0, 0)

        return pl.BlockSpec((None, depth, width), index)

    def out_spec(n):
        def index(s, p):
            return (jnp.where(s // 2 == n, s % 2, jnp.where(s // 2 < n, 0, 1)), 0, 0)

        return pl.BlockSpec((None, length, width), index)

    return pl.pallas_call(
        out_kernel,
        out_shape=[jax.ShapeDtypeStruct((2, length, width), jnp.bfloat16)] * 4,
        grid_spec=pltpu.PrefetchScalarGridSpec(
            num_scalar_prefetch=1,
            grid=(steps,),
            in_specs=[rows, rows, block_spec(0), block_spec(1)],
            out_specs=[out_spec(n % 2) for n in range(4)],
        ),
        compiler_params=pltpu.CompilerParams(vmem_limit_bytes=56 * 2**20),
        cost_estimate=pl.CostEstimate(
            flops=8 * length * depth * steps * width,
            bytes_accessed=2 * (4 * length * depth + 2 * steps * depth * width + 8 * length * width),
            transcendentals=0,
        ),
    )(place, mine, theirs, blocks, blocks)


def norm_kernel(text_ref, gain_ref, out_ref):
    values = text_ref[...].astype(jnp.float32)
    center = jnp.mean(values, axis=-1, keepdims=True)
    spread = jnp.mean(jnp.square(values - center), axis=-1, keepdims=True)
    normed = ((values - center) * lax.rsqrt(spread + 1e-05) * gain_ref[...]).astype(jnp.bfloat16)
    width = out_ref.shape[2] // NZ
    for n in range(2 * NZ):
        out_ref[n % 2, :, n // 2 * width : (n // 2 + 1) * width] = normed[:, n * width : (n + 1) * width]


def layer_norm(text_rows, norm_gain):
    length, model_width = text_rows.shape
    rows = 32
    return pl.pallas_call(
        norm_kernel,
        out_shape=jax.ShapeDtypeStruct((2, length, model_width // 2), jnp.bfloat16),
        grid=(length // rows,),
        in_specs=[
            pl.BlockSpec((rows, model_width), lambda s: (s, 0)),
            pl.BlockSpec((1, model_width), lambda s: (0, 0)),
        ],
        out_specs=pl.BlockSpec((2, rows, model_width // 2), lambda s: (0, s, 0)),
        compiler_params=pltpu.CompilerParams(vmem_limit_bytes=32 * 2**20),
        cost_estimate=pl.CostEstimate(
            flops=8 * length * model_width,
            bytes_accessed=4 * length * model_width,
            transcendentals=length,
        ),
    )(text_rows, norm_gain[None])


def attention_weights(queries, keys, token_image):
    length, head_width = queries.shape
    key_count = keys.shape[0]
    head_count = head_width // HEAD_DIM
    query_heads = queries.reshape(length, head_count, HEAD_DIM)
    key_heads = keys.reshape(key_count, head_count, HEAD_DIM)
    scores = jnp.einsum(
        "lhd,rhd->hlr", query_heads, key_heads, preferred_element_type=jnp.float32
    ) * HEAD_DIM ** (-0.5)
    blocks = lax.broadcasted_iota(jnp.int32, (key_count,), 0) // LATENTS
    visible = (blocks[None, :] <= token_image[:, None])[None, :, :]
    masked = jnp.where(visible, scores, -1e30)
    row_top = jnp.max(masked, axis=-1, keepdims=True)
    has_image = jnp.any(visible, axis=-1, keepdims=True)
    row_top = jnp.where(has_image, row_top, 0.0)
    exp_terms = jnp.where(visible, jnp.exp(masked - row_top), 0.0)
    denominator = jnp.sum(exp_terms, axis=-1, keepdims=True)
    return (exp_terms / jnp.maximum(denominator, 1.0)).astype(jnp.bfloat16)


def attend(weights, values):
    key_count, head_width = values.shape
    value_heads = values.reshape(key_count, head_width // HEAD_DIM, HEAD_DIM)
    attended = jnp.einsum("hlr,rhd->lhd", weights, value_heads, preferred_element_type=jnp.float32)
    return attended.astype(jnp.bfloat16).reshape(-1, head_width)


def to_final(piece, g):
    return permute(piece, lambda x, yh, c, yl, z: (yl * 2 + x % 2, yh ^ g, c, x // 2, z))


def total(own, moved):
    result = own.astype(jnp.float32)
    for part in moved:
        result = result + part.astype(jnp.float32)
    return result


def body(text_states, latents, norm_gain, w_query, w_key, w_value, w_out, xattn_gate, token_image):
    _, length, model_width = text_states.shape
    key_count = latents.shape[1]
    width = w_out.shape[1]
    section, place = lax.axis_index("section"), lax.axis_index("fsdp")
    x, yh, core, yl = section // 4, (section // 2) % 2, section % 2, place // NZ
    here = jnp.stack([x, yh * 2 + yl, core, yl, place % NZ]).astype(jnp.int32)

    latent_blocks = gather_plane(latents[0])
    latent_weights = ring_z(to_parity(jnp.stack([w_key, w_value])))
    one_away, two_away = (latent_weights[1], latent_weights[8]), (latent_weights[2], latent_weights[7])
    query_weights = gather_z(to_parity(after(w_query, *one_away)))
    out_weights = gather_z(swap_core_parity(after(w_out, *two_away)))

    normed = layer_norm(text_states[0], norm_gain)
    own_half = pick(normed, core)
    other_half = over_y(after(own_half, *one_away), 1)
    other_image = over_y(after(token_image, *two_away), 1)
    images = jnp.where(core == yl, token_image, other_image)[0]

    kept, sent = project_queries(here, normed, other_half, query_weights)
    queries = (kept + swap_cores(sent)).astype(jnp.bfloat16)
    kept, sent = project_latents(here, latent_blocks, latent_weights)
    keys, values = (kept + swap_cores(sent)).astype(jnp.bfloat16)
    attended = attend(attention_weights(queries, keys, images), values)

    mine = jnp.stack([attended, over_y(attended, 1)])
    parts = partial_sums(here, mine, swap_cores(mine), out_weights)
    near = total(parts[0], [over_x(parts[r], r) for r in (1, 2, 3)]).astype(jnp.bfloat16)
    projected = total(to_final(near[0], 0), [to_final(near[1], 1)])
    own_text = lax.dynamic_slice_in_dim(text_states[0], section * width, width, 1)
    mixed = own_text.astype(jnp.float32) + jnp.tanh(xattn_gate[0]) * projected
    return mixed.astype(jnp.bfloat16)[None]


def solution(mesh):
    in_specs = (
        P("fsdp", None, None),
        P("fsdp", None, "section"),
        P(),
        P("fsdp", "section"),
        P("fsdp", "section"),
        P("fsdp", "section"),
        P("section", "fsdp"),
        P(),
        P("fsdp", None),
    )
    out_specs = P("fsdp", None, "section")
    return jax.shard_map(body, mesh=mesh, in_specs=in_specs, out_specs=out_specs, check_vma=False)
```

```python
import jax
import jax.numpy as jnp
from jax import lax
from jax.experimental import pallas as pl
from jax.experimental.pallas import tpu as pltpu
from jax.sharding import PartitionSpec as P

HEAD_DIM = 128
LATENTS = 64
AXES = ("section", "fsdp")
NX, NYH, NC, NYL, NZ = 4, 2, 2, 2, 8


def permute(value, place):
    pairs = []
    for x in range(NX):
        for yh in range(NYH):
            for c in range(NC):
                for yl in range(NYL):
                    for z in range(NZ):
                        tx, tyh, tc, tyl, tz = place(x, yh, c, yl, z)
                        pairs.append(
                            (
                                (x * 4 + yh * 2 + c) * 16 + yl * 8 + z,
                                (tx * 4 + tyh * 2 + tc) * 16 + tyl * 8 + tz,
                            )
                        )
    return lax.ppermute(value, AXES, pairs)


def to_parity(value):
    return permute(value, lambda x, yh, c, yl, z: (x, yh, z % 2, c, z ^ yl ^ c))


def swap_core_parity(value):
    return permute(value, lambda x, yh, c, yl, z: (x, yh, z % 2, yl, z // 2 * 2 + c))


def swap_cores(value):
    return permute(value, lambda x, yh, c, yl, z: (x, yh, 1 - c, yl, z))


def over_x(value, r):
    return permute(value, lambda x, yh, c, yl, z: (x ^ r, yh, c, yl, z))


def along_x(value, step):
    return permute(value, lambda x, yh, c, yl, z: ((x + step) % NX, yh, c, yl, z))


def over_y(value, q):
    return permute(value, lambda x, yh, c, yl, z: (x, yh ^ (q >> 1), c, yl ^ (q & 1), z))


def pick(stacked, index):
    return lax.dynamic_index_in_dim(stacked, index, 0, keepdims=False)


def over_z(value, step):
    return permute(value, lambda x, yh, c, yl, z: (x, yh, c, yl, (z + step) % NZ))


def ring_z(shard):
    up, down = [shard], [shard]
    for _ in range(3):
        up.append(over_z(up[-1], 1))
        down.append(over_z(down[-1], -1))
    return down + [over_z(up[-1][:1], 1), over_z(down[-1][1:], -1)] + up[:0:-1]


def gather_z(value):
    groups = [list(range(NZ)), list(range(NZ, 2 * NZ))]
    return lax.all_gather(value, "fsdp", axis=0, axis_index_groups=groups)


def after(value, *earlier):
    return lax.optimization_barrier((value, *earlier))[0]


def gather_plane(block):
    groups = [
        [((y // 2) * 2 + x * 4 + core) * 16 + (y % 2) * NZ + z for x in range(NX) for y in range(4)]
        for z in range(NZ)
        for core in range(NC)
    ]
    return lax.all_gather(block, AXES, axis=0, axis_index_groups=groups)


def query_kernel(place_ref, own_ref, other_ref, weight_ref, kept, sent):
    @pl.when(pl.program_id(0) == 0)
    def _():
        kept[...] = jnp.zeros_like(kept)
        sent[...] = jnp.zeros_like(sent)

    weight = weight_ref[...]
    own = jnp.dot(own_ref[...], weight, preferred_element_type=jnp.float32)
    other = jnp.dot(other_ref[...], weight, preferred_element_type=jnp.float32)
    stays = place_ref[2] == place_ref[3]
    kept[...] += jnp.where(stays, own, other)
    sent[...] += jnp.where(stays, other, own)


def latent_kernel(place_ref, mine_0, mine_1, theirs_0, theirs_1, *refs):
    pieces, (kept, sent, held, sems) = refs[:9], refs[9:]
    k = pl.program_id(0)

    @pl.when(k == 0)
    def _():
        for n, piece in enumerate(pieces):
            if n in (4, 5):
                target, sem = held.at[4, pl.ds(n - 4, 1)], sems.at[4]
            else:
                target, sem = held.at[n - (n > 5)], sems.at[n - (n > 5)]
            pltpu.make_async_copy(piece, target, sem).start()

    at = []
    for j in range(2):
        d = (weight_at(2 * k + j, place_ref) - place_ref[4] + NZ) % NZ
        pltpu.make_async_copy(held.at[d], held.at[d], sems.at[d]).wait()
        at.append(d)
    for out, low, high in ((kept, mine_0, mine_1), (sent, theirs_0, theirs_1)):
        for n in range(2):
            sums = jnp.dot(low[...], held[at[0], n], preferred_element_type=jnp.float32) + jnp.dot(
                high[...], held[at[1], n], preferred_element_type=jnp.float32
            )

            @pl.when(k == 0)
            def _():
                out[n] = sums

            @pl.when(k > 0)
            def _():
                out[n] += sums


def weight_at(s, p):
    return s // 2 * 2 + ((s % 2) ^ p[2] ^ p[3])


def project_queries(place, normed, other_half, weights):
    length = normed.shape[1]
    steps, depth, width = weights.shape
    out = jax.ShapeDtypeStruct((length, width), jnp.float32)
    whole = pl.BlockSpec((length, width), lambda s, p: (0, 0))
    return pl.pallas_call(
        query_kernel,
        out_shape=(out, out),
        grid_spec=pltpu.PrefetchScalarGridSpec(
            num_scalar_prefetch=1,
            grid=(steps,),
            in_specs=[
                pl.BlockSpec((None, length, depth), lambda s, p: (p[2], 0, (s % 2) * 4 + s // 2)),
                pl.BlockSpec((length, depth), lambda s, p: (0, (s % 2) * 4 + s // 2)),
                pl.BlockSpec((None, depth, width), lambda s, p: (weight_at(s, p), 0, 0)),
            ],
            out_specs=(whole, whole),
        ),
        compiler_params=pltpu.CompilerParams(vmem_limit_bytes=16 * 2**20),
        cost_estimate=pl.CostEstimate(
            flops=4 * length * steps * depth * width,
            bytes_accessed=2 * steps * depth * (2 * length + width) + 8 * length * width,
            transcendentals=0,
        ),
    )(place, normed, other_half, weights)


def project_latents(place, latent_blocks, pieces):
    key_count = latent_blocks.shape[1]
    kinds, depth, width = pieces[0].shape

    def latent_spec(flip, j):
        def index(k, p):
            x_at, y_at = j * 2 + k // 2, (k % 2) * 2 + (p[2] + flip) % 2
            return (x_at * 4 + y_at, 0, 0)

        return pl.BlockSpec((None, key_count, depth), index)

    out = jax.ShapeDtypeStruct((kinds, key_count, width), jnp.float32)
    whole = pl.BlockSpec((kinds, key_count, width), lambda k, p: (0, 0, 0))
    return pl.pallas_call(
        latent_kernel,
        out_shape=(out, out),
        grid_spec=pltpu.PrefetchScalarGridSpec(
            num_scalar_prefetch=1,
            grid=(NZ // 2,),
            in_specs=[latent_spec(flip, j) for flip in range(2) for j in range(2)]
            + [pl.BlockSpec(memory_space=pl.ANY)] * len(pieces),
            out_specs=(whole, whole),
            scratch_shapes=[
                pltpu.VMEM((NZ, kinds, depth, width), jnp.bfloat16),
                pltpu.SemaphoreType.DMA((NZ,)),
            ],
        ),
        compiler_params=pltpu.CompilerParams(vmem_limit_bytes=26 * 2**20),
        cost_estimate=pl.CostEstimate(
            flops=4 * kinds * key_count * NZ * depth * width,
            bytes_accessed=2 * NZ * depth * (2 * key_count + kinds * width)
            + 8 * kinds * key_count * width,
            transcendentals=0,
        ),
    )(place, *[latent_blocks] * 4, *pieces)


def out_kernel(place_ref, mine_ref, theirs_ref, near_ref, far_ref, *parts):
    core, x_high = place_ref[2], place_ref[0] // 2

    def product(ref):
        return (
            jnp.dot(ref[0], near_ref[...], preferred_element_type=jnp.float32)
            + jnp.dot(ref[1], far_ref[...], preferred_element_type=jnp.float32)
        ).astype(jnp.bfloat16)

    mine, theirs = product(mine_ref), product(theirs_ref)
    near = jnp.where(core == x_high, mine, theirs)
    far = jnp.where(core == x_high, theirs, mine)
    for n in range(2):

        @pl.when(pl.program_id(0) // 2 == n)
        def _():
            parts[n][...] = near
            parts[2 + n][...] = far


def partial_sums(place, mine, theirs, blocks):
    _, length, depth = mine.shape
    steps, width = blocks.shape[0] // 2, blocks.shape[2]
    rows = pl.BlockSpec((2, length, depth), lambda s, p: (0, 0, 0))

    def block_spec(flip):
        def index(s, p):
            z = ((s // 2) ^ (p[0] % 2)) * 4 + ((s % 2) ^ (p[1] // 2)) * 2 + (p[3] ^ flip)
            return (z, 0, 0)

        return pl.BlockSpec((None, depth, width), index)

    def out_spec(n):
        def index(s, p):
            return (jnp.where(s // 2 == n, s % 2, jnp.where(s // 2 < n, 0, 1)), 0, 0)

        return pl.BlockSpec((None, length, width), index)

    return pl.pallas_call(
        out_kernel,
        out_shape=[jax.ShapeDtypeStruct((2, length, width), jnp.bfloat16)] * 4,
        grid_spec=pltpu.PrefetchScalarGridSpec(
            num_scalar_prefetch=1,
            grid=(steps,),
            in_specs=[rows, rows, block_spec(0), block_spec(1)],
            out_specs=[out_spec(n % 2) for n in range(4)],
        ),
        compiler_params=pltpu.CompilerParams(vmem_limit_bytes=16 * 2**20),
        cost_estimate=pl.CostEstimate(
            flops=8 * length * depth * steps * width,
            bytes_accessed=2 * (4 * length * depth + 2 * steps * depth * width + 8 * length * width),
            transcendentals=0,
        ),
    )(place, mine, theirs, blocks, blocks)


def norm_kernel(text_ref, gain_ref, out_ref):
    values = text_ref[...].astype(jnp.float32)
    center = jnp.mean(values, axis=-1, keepdims=True)
    spread = jnp.mean(jnp.square(values - center), axis=-1, keepdims=True)
    normed = ((values - center) * lax.rsqrt(spread + 1e-05) * gain_ref[...]).astype(jnp.bfloat16)
    width = out_ref.shape[2] // NZ
    for n in range(2 * NZ):
        out_ref[n % 2, :, n // 2 * width : (n // 2 + 1) * width] = normed[:, n * width : (n + 1) * width]


def layer_norm(text_rows, norm_gain):
    length, model_width = text_rows.shape
    rows = 32
    return pl.pallas_call(
        norm_kernel,
        out_shape=jax.ShapeDtypeStruct((2, length, model_width // 2), jnp.bfloat16),
        grid=(length // rows,),
        in_specs=[
            pl.BlockSpec((rows, model_width), lambda s: (s, 0)),
            pl.BlockSpec((1, model_width), lambda s: (0, 0)),
        ],
        out_specs=pl.BlockSpec((2, rows, model_width // 2), lambda s: (0, s, 0)),
        compiler_params=pltpu.CompilerParams(vmem_limit_bytes=32 * 2**20),
        cost_estimate=pl.CostEstimate(
            flops=8 * length * model_width,
            bytes_accessed=4 * length * model_width,
            transcendentals=length,
        ),
    )(text_rows, norm_gain[None])


def attention_weights(queries, keys, token_image):
    length, head_width = queries.shape
    key_count = keys.shape[0]
    head_count = head_width // HEAD_DIM
    query_heads = queries.reshape(length, head_count, HEAD_DIM)
    key_heads = keys.reshape(key_count, head_count, HEAD_DIM)
    scores = jnp.einsum(
        "lhd,rhd->hlr", query_heads, key_heads, preferred_element_type=jnp.float32
    ) * HEAD_DIM ** (-0.5)
    blocks = lax.broadcasted_iota(jnp.int32, (key_count,), 0) // LATENTS
    visible = (blocks[None, :] <= token_image[:, None])[None, :, :]
    masked = jnp.where(visible, scores, -1e30)
    row_top = jnp.max(masked, axis=-1, keepdims=True)
    has_image = jnp.any(visible, axis=-1, keepdims=True)
    row_top = jnp.where(has_image, row_top, 0.0)
    exp_terms = jnp.where(visible, jnp.exp(masked - row_top), 0.0)
    denominator = jnp.sum(exp_terms, axis=-1, keepdims=True)
    return (exp_terms / jnp.maximum(denominator, 1.0)).astype(jnp.bfloat16)


def attend(weights, values):
    key_count, head_width = values.shape
    value_heads = values.reshape(key_count, head_width // HEAD_DIM, HEAD_DIM)
    attended = jnp.einsum("hlr,rhd->lhd", weights, value_heads, preferred_element_type=jnp.float32)
    return attended.astype(jnp.bfloat16).reshape(-1, head_width)


def to_final(piece, g):
    return permute(piece, lambda x, yh, c, yl, z: (yl * 2 + x % 2, yh ^ g, c, x // 2, z))


def total(own, moved):
    result = own.astype(jnp.float32)
    for part in moved:
        result = result + part.astype(jnp.float32)
    return result


def body(text_states, latents, norm_gain, w_query, w_key, w_value, w_out, xattn_gate, token_image):
    _, length, model_width = text_states.shape
    key_count = latents.shape[1]
    width = w_out.shape[1]
    section, place = lax.axis_index("section"), lax.axis_index("fsdp")
    x, yh, core, yl = section // 4, (section // 2) % 2, section % 2, place // NZ
    here = jnp.stack([x, yh * 2 + yl, core, yl, place % NZ]).astype(jnp.int32)

    latent_blocks = gather_plane(latents[0])
    shards = to_parity(jnp.stack([w_key, w_value, w_query]))
    latent_weights = ring_z(shards[:2])
    one_away, two_away = (latent_weights[1], latent_weights[8]), (latent_weights[2], latent_weights[7])
    query_weights = gather_z(shards[2])
    out_weights = gather_z(after(swap_core_parity(after(w_out, shards)), *two_away))

    normed = layer_norm(text_states[0], norm_gain)
    own_half = pick(normed, core)
    other_half = over_y(after(own_half, *one_away), 1)
    other_image = over_y(after(token_image, *two_away), 1)
    images = jnp.where(core == yl, token_image, other_image)[0]

    kept, sent = project_latents(here, latent_blocks, latent_weights)
    received = swap_cores(sent)
    query_kept, query_sent = project_queries(here, normed, other_half, after(query_weights, sent))
    query_received = swap_cores(query_sent)
    keys, values = (kept + after(received, query_kept)).astype(jnp.bfloat16)
    queries = (query_kept + query_received).astype(jnp.bfloat16)
    attended = attend(attention_weights(queries, keys, images), values)

    mine = jnp.stack([attended, over_y(attended, 1)])
    parts = partial_sums(here, mine, swap_cores(mine), out_weights)
    near = total(parts[0], [over_x(parts[r], r) for r in (1, 2, 3)]).astype(jnp.bfloat16)
    projected = total(to_final(near[0], 0), [to_final(near[1], 1)])
    own_text = lax.dynamic_slice_in_dim(text_states[0], section * width, width, 1)
    mixed = own_text.astype(jnp.float32) + jnp.tanh(xattn_gate[0]) * projected
    return mixed.astype(jnp.bfloat16)[None]


def solution(mesh):
    in_specs = (
        P("fsdp", None, None),
        P("fsdp", None, "section"),
        P(),
        P("fsdp", "section"),
        P("fsdp", "section"),
        P("fsdp", "section"),
        P("section", "fsdp"),
        P(),
        P("fsdp", None),
    )
    out_specs = P("fsdp", None, "section")
    return jax.shard_map(body, mesh=mesh, in_specs=in_specs, out_specs=out_specs, check_vma=False)
```

```python
import jax
import jax.numpy as jnp
from jax import lax
from jax.experimental import pallas as pl
from jax.experimental.pallas import tpu as pltpu
from jax.sharding import PartitionSpec as P

HEAD_DIM = 128
LATENTS = 64
AXES = ("section", "fsdp")
NX, NYH, NC, NYL, NZ = 4, 2, 2, 2, 8


def permute(value, place):
    pairs = []
    for x in range(NX):
        for yh in range(NYH):
            for c in range(NC):
                for yl in range(NYL):
                    for z in range(NZ):
                        tx, tyh, tc, tyl, tz = place(x, yh, c, yl, z)
                        pairs.append(
                            (
                                (x * 4 + yh * 2 + c) * 16 + yl * 8 + z,
                                (tx * 4 + tyh * 2 + tc) * 16 + tyl * 8 + tz,
                            )
                        )
    return lax.ppermute(value, AXES, pairs)


def to_parity(value):
    return permute(value, lambda x, yh, c, yl, z: (x, yh, z % 2, c, z ^ yl ^ c))


def swap_core_parity(value):
    return permute(value, lambda x, yh, c, yl, z: (x, yh, z % 2, yl, z // 2 * 2 + c))


def swap_cores(value):
    return permute(value, lambda x, yh, c, yl, z: (x, yh, 1 - c, yl, z))


def over_x(value, r):
    return permute(value, lambda x, yh, c, yl, z: (x ^ r, yh, c, yl, z))


def along_x(value, step):
    return permute(value, lambda x, yh, c, yl, z: ((x + step) % NX, yh, c, yl, z))


def over_y(value, q):
    return permute(value, lambda x, yh, c, yl, z: (x, yh ^ (q >> 1), c, yl ^ (q & 1), z))


def pick(stacked, index):
    return lax.dynamic_index_in_dim(stacked, index, 0, keepdims=False)


def over_z(value, step):
    return permute(value, lambda x, yh, c, yl, z: (x, yh, c, yl, (z + step) % NZ))


def ring_z(shard):
    up, down = [shard], [shard]
    for _ in range(3):
        up.append(over_z(up[-1], 1))
        down.append(over_z(down[-1], -1))
    return down + [over_z(up[-1][:1], 1), over_z(down[-1][1:], -1)] + up[:0:-1]


def gather_z(value):
    groups = [list(range(NZ)), list(range(NZ, 2 * NZ))]
    return lax.all_gather(value, "fsdp", axis=0, axis_index_groups=groups)


def after(value, *earlier):
    return lax.optimization_barrier((value, *earlier))[0]


def gather_plane(block):
    groups = [
        [((y // 2) * 2 + x * 4 + core) * 16 + (y % 2) * NZ + z for x in range(NX) for y in range(4)]
        for z in range(NZ)
        for core in range(NC)
    ]
    return lax.all_gather(block, AXES, axis=0, axis_index_groups=groups)


def query_kernel(place_ref, own_ref, other_ref, weight_ref, kept, sent):
    @pl.when(pl.program_id(0) == 0)
    def _():
        kept[...] = jnp.zeros_like(kept)
        sent[...] = jnp.zeros_like(sent)

    weight = weight_ref[...]
    own = jnp.dot(own_ref[...], weight, preferred_element_type=jnp.float32)
    other = jnp.dot(other_ref[...], weight, preferred_element_type=jnp.float32)
    stays = place_ref[2] == place_ref[3]
    kept[...] += jnp.where(stays, own, other)
    sent[...] += jnp.where(stays, other, own)


def latent_kernel(place_ref, mine_0, mine_1, theirs_0, theirs_1, *refs):
    pieces, (kept, sent, held, sems) = refs[:9], refs[9:]
    k = pl.program_id(0)

    @pl.when(k == 0)
    def _():
        for n, piece in enumerate(pieces):
            if n in (4, 5):
                target, sem = held.at[4, pl.ds(n - 4, 1)], sems.at[4]
            else:
                target, sem = held.at[n - (n > 5)], sems.at[n - (n > 5)]
            pltpu.make_async_copy(piece, target, sem).start()

    at = []
    for j in range(2):
        d = (weight_at(2 * k + j, place_ref) - place_ref[4] + NZ) % NZ
        pltpu.make_async_copy(held.at[d], held.at[d], sems.at[d]).wait()
        at.append(d)
    for out, low, high in ((kept, mine_0, mine_1), (sent, theirs_0, theirs_1)):
        for n in range(2):
            sums = jnp.dot(low[...], held[at[0], n], preferred_element_type=jnp.float32) + jnp.dot(
                high[...], held[at[1], n], preferred_element_type=jnp.float32
            )

            @pl.when(k == 0)
            def _():
                out[n] = sums

            @pl.when(k > 0)
            def _():
                out[n] += sums


def weight_at(s, p):
    return s // 2 * 2 + ((s % 2) ^ p[2] ^ p[3])


def project_queries(place, normed, other_half, weights):
    length = normed.shape[1]
    steps, depth, width = weights.shape
    out = jax.ShapeDtypeStruct((length, width), jnp.float32)
    whole = pl.BlockSpec((length, width), lambda s, p: (0, 0))
    return pl.pallas_call(
        query_kernel,
        out_shape=(out, out),
        grid_spec=pltpu.PrefetchScalarGridSpec(
            num_scalar_prefetch=1,
            grid=(steps,),
            in_specs=[
                pl.BlockSpec((None, length, depth), lambda s, p: (p[2], 0, (s % 2) * 4 + s // 2)),
                pl.BlockSpec((length, depth), lambda s, p: (0, (s % 2) * 4 + s // 2)),
                pl.BlockSpec((None, depth, width), lambda s, p: (weight_at(s, p), 0, 0)),
            ],
            out_specs=(whole, whole),
        ),
        compiler_params=pltpu.CompilerParams(vmem_limit_bytes=16 * 2**20),
        cost_estimate=pl.CostEstimate(
            flops=4 * length * steps * depth * width,
            bytes_accessed=2 * steps * depth * (2 * length + width) + 8 * length * width,
            transcendentals=0,
        ),
    )(place, normed, other_half, weights)


def project_latents(place, latent_blocks, pieces):
    key_count = latent_blocks.shape[1]
    kinds, depth, width = pieces[0].shape

    def latent_spec(flip, j):
        def index(k, p):
            x_at, y_at = j * 2 + k // 2, (k % 2) * 2 + (p[2] + flip) % 2
            return (x_at * 4 + y_at, 0, 0)

        return pl.BlockSpec((None, key_count, depth), index)

    out = jax.ShapeDtypeStruct((kinds, key_count, width), jnp.float32)
    whole = pl.BlockSpec((kinds, key_count, width), lambda k, p: (0, 0, 0))
    return pl.pallas_call(
        latent_kernel,
        out_shape=(out, out),
        grid_spec=pltpu.PrefetchScalarGridSpec(
            num_scalar_prefetch=1,
            grid=(NZ // 2,),
            in_specs=[latent_spec(flip, j) for flip in range(2) for j in range(2)]
            + [pl.BlockSpec(memory_space=pl.ANY)] * len(pieces),
            out_specs=(whole, whole),
            scratch_shapes=[
                pltpu.VMEM((NZ, kinds, depth, width), jnp.bfloat16),
                pltpu.SemaphoreType.DMA((NZ,)),
            ],
        ),
        compiler_params=pltpu.CompilerParams(vmem_limit_bytes=26 * 2**20),
        cost_estimate=pl.CostEstimate(
            flops=4 * kinds * key_count * NZ * depth * width,
            bytes_accessed=2 * NZ * depth * (2 * key_count + kinds * width)
            + 8 * kinds * key_count * width,
            transcendentals=0,
        ),
    )(place, *[latent_blocks] * 4, *pieces)


def out_kernel(place_ref, mine_ref, theirs_ref, near_ref, far_ref, *parts):
    core, x_high = place_ref[2], place_ref[0] // 2
    cut = near_ref.shape[1] // 2

    def product(ref):
        return (
            jnp.dot(ref[0], near_ref[...], preferred_element_type=jnp.float32)
            + jnp.dot(ref[1], far_ref[...], preferred_element_type=jnp.float32)
        ).astype(jnp.bfloat16)

    mine, theirs = product(mine_ref), product(theirs_ref)
    near = jnp.where(core == x_high, mine, theirs)
    far = jnp.where(core == x_high, theirs, mine)
    for n in range(2):

        @pl.when(pl.program_id(0) // 2 == n)
        def _():
            for half in range(2):
                columns = slice(half * cut, (half + 1) * cut)
                parts[4 * half + n][...] = near[:, columns]
                parts[4 * half + 2 + n][...] = far[:, columns]


def partial_sums(place, mine, theirs, blocks):
    _, length, depth = mine.shape
    steps, width = blocks.shape[0] // 2, blocks.shape[2]
    rows = pl.BlockSpec((2, length, depth), lambda s, p: (0, 0, 0))

    def block_spec(flip):
        def index(s, p):
            z = ((s // 2) ^ (p[0] % 2)) * 4 + ((s % 2) ^ (p[1] // 2)) * 2 + (p[3] ^ flip)
            return (z, 0, 0)

        return pl.BlockSpec((None, depth, width), index)

    def out_spec(n):
        def index(s, p):
            return (jnp.where(s // 2 == n, s % 2, jnp.where(s // 2 < n, 0, 1)), 0, 0)

        return pl.BlockSpec((None, length, width // 2), index)

    return pl.pallas_call(
        out_kernel,
        out_shape=[jax.ShapeDtypeStruct((2, length, width // 2), jnp.bfloat16)] * 8,
        grid_spec=pltpu.PrefetchScalarGridSpec(
            num_scalar_prefetch=1,
            grid=(steps,),
            in_specs=[rows, rows, block_spec(0), block_spec(1)],
            out_specs=[out_spec(n % 2) for n in range(8)],
        ),
        compiler_params=pltpu.CompilerParams(vmem_limit_bytes=16 * 2**20),
        cost_estimate=pl.CostEstimate(
            flops=8 * length * depth * steps * width,
            bytes_accessed=2 * (4 * length * depth + 2 * steps * depth * width + 8 * length * width),
            transcendentals=0,
        ),
    )(place, mine, theirs, blocks, blocks)


def norm_kernel(text_ref, gain_ref, out_ref):
    values = text_ref[...].astype(jnp.float32)
    center = jnp.mean(values, axis=-1, keepdims=True)
    spread = jnp.mean(jnp.square(values - center), axis=-1, keepdims=True)
    normed = ((values - center) * lax.rsqrt(spread + 1e-05) * gain_ref[...]).astype(jnp.bfloat16)
    width = out_ref.shape[2] // NZ
    for n in range(2 * NZ):
        out_ref[n % 2, :, n // 2 * width : (n // 2 + 1) * width] = normed[:, n * width : (n + 1) * width]


def layer_norm(text_rows, norm_gain):
    length, model_width = text_rows.shape
    rows = 32
    return pl.pallas_call(
        norm_kernel,
        out_shape=jax.ShapeDtypeStruct((2, length, model_width // 2), jnp.bfloat16),
        grid=(length // rows,),
        in_specs=[
            pl.BlockSpec((rows, model_width), lambda s: (s, 0)),
            pl.BlockSpec((1, model_width), lambda s: (0, 0)),
        ],
        out_specs=pl.BlockSpec((2, rows, model_width // 2), lambda s: (0, s, 0)),
        compiler_params=pltpu.CompilerParams(vmem_limit_bytes=32 * 2**20),
        cost_estimate=pl.CostEstimate(
            flops=8 * length * model_width,
            bytes_accessed=4 * length * model_width,
            transcendentals=length,
        ),
    )(text_rows, norm_gain[None])


def attention_weights(queries, keys, token_image):
    length, head_width = queries.shape
    key_count = keys.shape[0]
    head_count = head_width // HEAD_DIM
    query_heads = queries.reshape(length, head_count, HEAD_DIM)
    key_heads = keys.reshape(key_count, head_count, HEAD_DIM)
    scores = jnp.einsum(
        "lhd,rhd->hlr", query_heads, key_heads, preferred_element_type=jnp.float32
    ) * HEAD_DIM ** (-0.5)
    blocks = lax.broadcasted_iota(jnp.int32, (key_count,), 0) // LATENTS
    visible = (blocks[None, :] <= token_image[:, None])[None, :, :]
    masked = jnp.where(visible, scores, -1e30)
    row_top = jnp.max(masked, axis=-1, keepdims=True)
    has_image = jnp.any(visible, axis=-1, keepdims=True)
    row_top = jnp.where(has_image, row_top, 0.0)
    exp_terms = jnp.where(visible, jnp.exp(masked - row_top), 0.0)
    denominator = jnp.sum(exp_terms, axis=-1, keepdims=True)
    return (exp_terms / jnp.maximum(denominator, 1.0)).astype(jnp.bfloat16)


def attend(weights, values):
    key_count, head_width = values.shape
    value_heads = values.reshape(key_count, head_width // HEAD_DIM, HEAD_DIM)
    attended = jnp.einsum("hlr,rhd->lhd", weights, value_heads, preferred_element_type=jnp.float32)
    return attended.astype(jnp.bfloat16).reshape(-1, head_width)


def to_final(piece, g):
    return permute(piece, lambda x, yh, c, yl, z: (yl * 2 + x % 2, yh ^ g, c, x // 2, z))


def total(own, moved):
    result = own.astype(jnp.float32)
    for part in moved:
        result = result + part.astype(jnp.float32)
    return result


def body(text_states, latents, norm_gain, w_query, w_key, w_value, w_out, xattn_gate, token_image):
    _, length, model_width = text_states.shape
    key_count = latents.shape[1]
    width = w_out.shape[1]
    section, place = lax.axis_index("section"), lax.axis_index("fsdp")
    x, yh, core, yl = section // 4, (section // 2) % 2, section % 2, place // NZ
    here = jnp.stack([x, yh * 2 + yl, core, yl, place % NZ]).astype(jnp.int32)

    latent_blocks = gather_plane(latents[0])
    shards = to_parity(jnp.stack([w_key, w_value, w_query]))
    latent_weights = ring_z(shards[:2])
    one_away, two_away = (latent_weights[1], latent_weights[8]), (latent_weights[2], latent_weights[7])
    query_weights = gather_z(shards[2])
    out_weights = gather_z(after(swap_core_parity(after(w_out, shards)), *two_away))

    normed = layer_norm(text_states[0], norm_gain)
    own_half = pick(normed, core)
    other_half = over_y(after(own_half, *one_away), 1)
    other_image = over_y(after(token_image, *two_away), 1)
    images = jnp.where(core == yl, token_image, other_image)[0]

    kept, sent = project_latents(here, latent_blocks, latent_weights)
    received = swap_cores(sent)
    query_kept, query_sent = project_queries(here, normed, other_half, after(query_weights, sent))
    query_received = swap_cores(query_sent)
    keys, values = (kept + after(received, query_kept)).astype(jnp.bfloat16)
    queries = (query_kept + query_received).astype(jnp.bfloat16)
    attended = attend(attention_weights(queries, keys, images), values)

    mine = jnp.stack([attended, over_y(attended, 1)])
    parts = partial_sums(here, mine, swap_cores(mine), out_weights)
    halves = []
    for own, *others in (parts[:4], parts[4:]):
        near = total(own, [over_x(others[r - 1], r) for r in (1, 2, 3)]).astype(jnp.bfloat16)
        halves.append(total(to_final(near[0], 0), [to_final(near[1], 1)]))
    projected = jnp.concatenate(halves, axis=1)
    own_text = lax.dynamic_slice_in_dim(text_states[0], section * width, width, 1)
    mixed = own_text.astype(jnp.float32) + jnp.tanh(xattn_gate[0]) * projected
    return mixed.astype(jnp.bfloat16)[None]


def solution(mesh):
    in_specs = (
        P("fsdp", None, None),
        P("fsdp", None, "section"),
        P(),
        P("fsdp", "section"),
        P("fsdp", "section"),
        P("fsdp", "section"),
        P("section", "fsdp"),
        P(),
        P("fsdp", None),
    )
    out_specs = P("fsdp", None, "section")
    return jax.shard_map(body, mesh=mesh, in_specs=in_specs, out_specs=out_specs, check_vma=False)
```

```python
import jax
import jax.numpy as jnp
from jax import lax
from jax.experimental import pallas as pl
from jax.experimental.pallas import tpu as pltpu
from jax.sharding import PartitionSpec as P

HEAD_DIM = 128
LATENTS = 64
AXES = ("section", "fsdp")
NX, NYH, NC, NYL, NZ = 4, 2, 2, 2, 8


def permute(value, place):
    pairs = []
    for x in range(NX):
        for yh in range(NYH):
            for c in range(NC):
                for yl in range(NYL):
                    for z in range(NZ):
                        tx, tyh, tc, tyl, tz = place(x, yh, c, yl, z)
                        pairs.append(
                            (
                                (x * 4 + yh * 2 + c) * 16 + yl * 8 + z,
                                (tx * 4 + tyh * 2 + tc) * 16 + tyl * 8 + tz,
                            )
                        )
    return lax.ppermute(value, AXES, pairs)


def to_parity(value):
    return permute(value, lambda x, yh, c, yl, z: (x, yh, z % 2, c, z ^ yl ^ c))


def swap_core_parity(value):
    return permute(value, lambda x, yh, c, yl, z: (x, yh, z % 2, yl, z // 2 * 2 + c))


def swap_cores(value):
    return permute(value, lambda x, yh, c, yl, z: (x, yh, 1 - c, yl, z))


def over_x(value, r):
    return permute(value, lambda x, yh, c, yl, z: (x ^ r, yh, c, yl, z))


def along_x(value, step):
    return permute(value, lambda x, yh, c, yl, z: ((x + step) % NX, yh, c, yl, z))


def over_y(value, q):
    return permute(value, lambda x, yh, c, yl, z: (x, yh ^ (q >> 1), c, yl ^ (q & 1), z))


def pick(stacked, index):
    return lax.dynamic_index_in_dim(stacked, index, 0, keepdims=False)


def over_z(value, step):
    return permute(value, lambda x, yh, c, yl, z: (x, yh, c, yl, (z + step) % NZ))


def ring_z(shard):
    up, down = [shard], [shard]
    for _ in range(3):
        up.append(over_z(up[-1], 1))
        down.append(over_z(down[-1], -1))
    return down + [over_z(up[-1][:1], 1), over_z(down[-1][1:], -1)] + up[:0:-1]


def gather_z(value):
    groups = [list(range(NZ)), list(range(NZ, 2 * NZ))]
    return lax.all_gather(value, "fsdp", axis=0, axis_index_groups=groups)


def after(value, *earlier):
    return lax.optimization_barrier((value, *earlier))[0]


def gather_plane(block):
    groups = [
        [((y // 2) * 2 + x * 4 + core) * 16 + (y % 2) * NZ + z for x in range(NX) for y in range(4)]
        for z in range(NZ)
        for core in range(NC)
    ]
    return lax.all_gather(block, AXES, axis=0, axis_index_groups=groups)


def query_kernel(place_ref, own_ref, other_ref, weight_ref, kept, sent):
    @pl.when(pl.program_id(0) == 0)
    def _():
        kept[...] = jnp.zeros_like(kept)
        sent[...] = jnp.zeros_like(sent)

    weight = weight_ref[...]
    own = jnp.dot(own_ref[...], weight, preferred_element_type=jnp.float32)
    other = jnp.dot(other_ref[...], weight, preferred_element_type=jnp.float32)
    stays = place_ref[2] == place_ref[3]
    kept[...] += jnp.where(stays, own, other)
    sent[...] += jnp.where(stays, other, own)


def latent_kernel(place_ref, mine_0, mine_1, theirs_0, theirs_1, *refs):
    pieces, (kept, sent, held, sems) = refs[:9], refs[9:]
    k = pl.program_id(0)

    @pl.when(k == 0)
    def _():
        for n, piece in enumerate(pieces):
            if n in (4, 5):
                target, sem = held.at[4, pl.ds(n - 4, 1)], sems.at[4]
            else:
                target, sem = held.at[n - (n > 5)], sems.at[n - (n > 5)]
            pltpu.make_async_copy(piece, target, sem).start()

    at = []
    for j in range(2):
        d = (weight_at(2 * k + j, place_ref) - place_ref[4] + NZ) % NZ
        pltpu.make_async_copy(held.at[d], held.at[d], sems.at[d]).wait()
        at.append(d)
    for out, low, high in ((kept, mine_0, mine_1), (sent, theirs_0, theirs_1)):
        for n in range(2):
            sums = jnp.dot(low[...], held[at[0], n], preferred_element_type=jnp.float32) + jnp.dot(
                high[...], held[at[1], n], preferred_element_type=jnp.float32
            )

            @pl.when(k == 0)
            def _():
                out[n] = sums

            @pl.when(k > 0)
            def _():
                out[n] += sums


def weight_at(s, p):
    return s // 2 * 2 + ((s % 2) ^ p[2] ^ p[3])


def project_queries(place, normed, other_half, weights):
    length = normed.shape[1]
    steps, depth, width = weights.shape
    out = jax.ShapeDtypeStruct((length, width), jnp.float32)
    whole = pl.BlockSpec((length, width), lambda s, p: (0, 0))
    return pl.pallas_call(
        query_kernel,
        out_shape=(out, out),
        grid_spec=pltpu.PrefetchScalarGridSpec(
            num_scalar_prefetch=1,
            grid=(steps,),
            in_specs=[
                pl.BlockSpec((None, length, depth), lambda s, p: (p[2], 0, (s % 2) * 4 + s // 2)),
                pl.BlockSpec((length, depth), lambda s, p: (0, (s % 2) * 4 + s // 2)),
                pl.BlockSpec((None, depth, width), lambda s, p: (weight_at(s, p), 0, 0)),
            ],
            out_specs=(whole, whole),
        ),
        compiler_params=pltpu.CompilerParams(vmem_limit_bytes=16 * 2**20),
        cost_estimate=pl.CostEstimate(
            flops=4 * length * steps * depth * width,
            bytes_accessed=2 * steps * depth * (2 * length + width) + 8 * length * width,
            transcendentals=0,
        ),
    )(place, normed, other_half, weights)


def project_latents(place, latent_blocks, pieces):
    key_count = latent_blocks.shape[1]
    kinds, depth, width = pieces[0].shape

    def latent_spec(flip, j):
        def index(k, p):
            x_at, y_at = j * 2 + k // 2, (k % 2) * 2 + (p[2] + flip) % 2
            return (x_at * 4 + y_at, 0, 0)

        return pl.BlockSpec((None, key_count, depth), index)

    out = jax.ShapeDtypeStruct((kinds, key_count, width), jnp.float32)
    whole = pl.BlockSpec((kinds, key_count, width), lambda k, p: (0, 0, 0))
    return pl.pallas_call(
        latent_kernel,
        out_shape=(out, out),
        grid_spec=pltpu.PrefetchScalarGridSpec(
            num_scalar_prefetch=1,
            grid=(NZ // 2,),
            in_specs=[latent_spec(flip, j) for flip in range(2) for j in range(2)]
            + [pl.BlockSpec(memory_space=pl.ANY)] * len(pieces),
            out_specs=(whole, whole),
            scratch_shapes=[
                pltpu.VMEM((NZ, kinds, depth, width), jnp.bfloat16),
                pltpu.SemaphoreType.DMA((NZ,)),
            ],
        ),
        compiler_params=pltpu.CompilerParams(vmem_limit_bytes=26 * 2**20),
        cost_estimate=pl.CostEstimate(
            flops=4 * kinds * key_count * NZ * depth * width,
            bytes_accessed=2 * NZ * depth * (2 * key_count + kinds * width)
            + 8 * kinds * key_count * width,
            transcendentals=0,
        ),
    )(place, *[latent_blocks] * 4, *pieces)


def out_kernel(place_ref, mine_ref, theirs_ref, near_ref, far_ref, *parts):
    core, x_high = place_ref[2], place_ref[0] // 2
    cut = parts[0].shape[1]

    def product(ref):
        return (
            jnp.dot(ref[0], near_ref[...], preferred_element_type=jnp.float32)
            + jnp.dot(ref[1], far_ref[...], preferred_element_type=jnp.float32)
        ).astype(jnp.bfloat16)

    mine, theirs = product(mine_ref), product(theirs_ref)
    near = jnp.where(core == x_high, mine, theirs)
    far = jnp.where(core == x_high, theirs, mine)
    for n in range(2):

        @pl.when(pl.program_id(0) // 2 == n)
        def _():
            for half in range(2):
                columns = slice(cut, None) if half else slice(0, cut)
                parts[4 * half + n][...] = near[:, columns]
                parts[4 * half + 2 + n][...] = far[:, columns]


def partial_sums(place, mine, theirs, blocks):
    _, length, depth = mine.shape
    steps, width = blocks.shape[0] // 2, blocks.shape[2]
    rows = pl.BlockSpec((2, length, depth), lambda s, p: (0, 0, 0))

    def block_spec(flip):
        def index(s, p):
            z = ((s // 2) ^ (p[0] % 2)) * 4 + ((s % 2) ^ (p[1] // 2)) * 2 + (p[3] ^ flip)
            return (z, 0, 0)

        return pl.BlockSpec((None, depth, width), index)

    cuts = [3 * width // 4] * 4 + [width // 4] * 4

    def out_spec(n, cut):
        def index(s, p):
            return (jnp.where(s // 2 == n, s % 2, jnp.where(s // 2 < n, 0, 1)), 0, 0)

        return pl.BlockSpec((None, length, cut), index)

    return pl.pallas_call(
        out_kernel,
        out_shape=[jax.ShapeDtypeStruct((2, length, cut), jnp.bfloat16) for cut in cuts],
        grid_spec=pltpu.PrefetchScalarGridSpec(
            num_scalar_prefetch=1,
            grid=(steps,),
            in_specs=[rows, rows, block_spec(0), block_spec(1)],
            out_specs=[out_spec(n % 2, cut) for n, cut in enumerate(cuts)],
        ),
        compiler_params=pltpu.CompilerParams(vmem_limit_bytes=16 * 2**20),
        cost_estimate=pl.CostEstimate(
            flops=8 * length * depth * steps * width,
            bytes_accessed=2 * (4 * length * depth + 2 * steps * depth * width + 8 * length * width),
            transcendentals=0,
        ),
    )(place, mine, theirs, blocks, blocks)


def norm_kernel(text_ref, gain_ref, out_ref):
    values = text_ref[...].astype(jnp.float32)
    center = jnp.mean(values, axis=-1, keepdims=True)
    spread = jnp.mean(jnp.square(values - center), axis=-1, keepdims=True)
    normed = ((values - center) * lax.rsqrt(spread + 1e-05) * gain_ref[...]).astype(jnp.bfloat16)
    width = out_ref.shape[2] // NZ
    for n in range(2 * NZ):
        out_ref[n % 2, :, n // 2 * width : (n // 2 + 1) * width] = normed[:, n * width : (n + 1) * width]


def layer_norm(text_rows, norm_gain):
    length, model_width = text_rows.shape
    rows = 32
    return pl.pallas_call(
        norm_kernel,
        out_shape=jax.ShapeDtypeStruct((2, length, model_width // 2), jnp.bfloat16),
        grid=(length // rows,),
        in_specs=[
            pl.BlockSpec((rows, model_width), lambda s: (s, 0)),
            pl.BlockSpec((1, model_width), lambda s: (0, 0)),
        ],
        out_specs=pl.BlockSpec((2, rows, model_width // 2), lambda s: (0, s, 0)),
        compiler_params=pltpu.CompilerParams(vmem_limit_bytes=32 * 2**20),
        cost_estimate=pl.CostEstimate(
            flops=8 * length * model_width,
            bytes_accessed=4 * length * model_width,
            transcendentals=length,
        ),
    )(text_rows, norm_gain[None])


def attention_weights(queries, keys, token_image):
    length, head_width = queries.shape
    key_count = keys.shape[0]
    head_count = head_width // HEAD_DIM
    query_heads = queries.reshape(length, head_count, HEAD_DIM)
    key_heads = keys.reshape(key_count, head_count, HEAD_DIM)
    scores = jnp.einsum(
        "lhd,rhd->hlr", query_heads, key_heads, preferred_element_type=jnp.float32
    ) * HEAD_DIM ** (-0.5)
    blocks = lax.broadcasted_iota(jnp.int32, (key_count,), 0) // LATENTS
    visible = (blocks[None, :] <= token_image[:, None])[None, :, :]
    masked = jnp.where(visible, scores, -1e30)
    row_top = jnp.max(masked, axis=-1, keepdims=True)
    has_image = jnp.any(visible, axis=-1, keepdims=True)
    row_top = jnp.where(has_image, row_top, 0.0)
    exp_terms = jnp.where(visible, jnp.exp(masked - row_top), 0.0)
    denominator = jnp.sum(exp_terms, axis=-1, keepdims=True)
    return (exp_terms / jnp.maximum(denominator, 1.0)).astype(jnp.bfloat16)


def attend(weights, values):
    key_count, head_width = values.shape
    value_heads = values.reshape(key_count, head_width // HEAD_DIM, HEAD_DIM)
    attended = jnp.einsum("hlr,rhd->lhd", weights, value_heads, preferred_element_type=jnp.float32)
    return attended.astype(jnp.bfloat16).reshape(-1, head_width)


def to_final(piece, g):
    return permute(piece, lambda x, yh, c, yl, z: (yl * 2 + x % 2, yh ^ g, c, x // 2, z))


def total(own, moved):
    result = own.astype(jnp.float32)
    for part in moved:
        result = result + part.astype(jnp.float32)
    return result


def body(text_states, latents, norm_gain, w_query, w_key, w_value, w_out, xattn_gate, token_image):
    _, length, model_width = text_states.shape
    key_count = latents.shape[1]
    width = w_out.shape[1]
    section, place = lax.axis_index("section"), lax.axis_index("fsdp")
    x, yh, core, yl = section // 4, (section // 2) % 2, section % 2, place // NZ
    here = jnp.stack([x, yh * 2 + yl, core, yl, place % NZ]).astype(jnp.int32)

    latent_blocks = gather_plane(latents[0])
    shards = to_parity(jnp.stack([w_key, w_value, w_query]))
    latent_weights = ring_z(shards[:2])
    one_away, two_away = (latent_weights[1], latent_weights[8]), (latent_weights[2], latent_weights[7])
    query_weights = gather_z(shards[2])
    out_weights = gather_z(after(swap_core_parity(after(w_out, shards)), *two_away))

    normed = layer_norm(text_states[0], norm_gain)
    own_half = pick(normed, core)
    other_half = over_y(after(own_half, *one_away), 1)
    other_image = over_y(after(token_image, *two_away), 1)
    images = jnp.where(core == yl, token_image, other_image)[0]

    kept, sent = project_latents(here, latent_blocks, latent_weights)
    received = swap_cores(sent)
    query_kept, query_sent = project_queries(here, normed, other_half, after(query_weights, sent))
    query_received = swap_cores(query_sent)
    keys, values = (kept + after(received, query_kept)).astype(jnp.bfloat16)
    queries = (query_kept + query_received).astype(jnp.bfloat16)
    attended = attend(attention_weights(queries, keys, images), values)

    mine = jnp.stack([attended, over_y(attended, 1)])
    parts = partial_sums(here, mine, swap_cores(mine), out_weights)
    halves = []
    for own, *others in (parts[:4], parts[4:]):
        near = total(own, [over_x(others[r - 1], r) for r in (1, 2, 3)]).astype(jnp.bfloat16)
        halves.append(total(to_final(near[0], 0), [to_final(near[1], 1)]))
    projected = jnp.concatenate(halves, axis=1)
    own_text = lax.dynamic_slice_in_dim(text_states[0], section * width, width, 1)
    mixed = own_text.astype(jnp.float32) + jnp.tanh(xattn_gate[0]) * projected
    return mixed.astype(jnp.bfloat16)[None]


def solution(mesh):
    in_specs = (
        P("fsdp", None, None),
        P("fsdp", None, "section"),
        P(),
        P("fsdp", "section"),
        P("fsdp", "section"),
        P("fsdp", "section"),
        P("section", "fsdp"),
        P(),
        P("fsdp", None),
    )
    out_specs = P("fsdp", None, "section")
    return jax.shard_map(body, mesh=mesh, in_specs=in_specs, out_specs=out_specs, check_vma=False)
```
